32 devices in a mesh: groups: 2 (over x), dp: 16 (over z, y, core).
Axes of the slice: x: 2, y: 2, z: 4, core: 2. Of those that a mesh axis runs over, the one named last changes fastest.
Arguments:
- tokens: bfloat16 [8192, 8192], P(('groups', 'dp')), parts along dimension 0, may hold values from -6 to 6
- chosen_rows: bfloat16 [8192, 8192], P(('groups', 'dp')), parts along dimension 0, may hold values from -0.0625 to 0.0625
- adapter_down: bfloat16 [8192, 256], P('dp'), may hold values from -0.0625 to 0.0625
- adapter_up: bfloat16 [256, 8192], P(None, 'dp'), may hold values from -0.375 to 0.375
- lengths: int32 [32], P(('groups', 'dp')), parts along dimension 0, may hold values from 1 to 256
- parent: int32 [32], P(('groups', 'dp')), parts along dimension 0, may hold values from 0 to 7
- depth: int32 [32], P(('groups', 'dp')), parts along dimension 0, may hold values from 0 to 7
- reward: float32 [32], P(('groups', 'dp')), parts along dimension 0, may hold values from -6 to 6
Outputs:
- grad_down: float32 [16384, 256], P(('groups', 'dp')), parts along dimension 0
- grad_up: float32 [512, 8192], P('groups', 'dp'), parts along dimension 0
- advantage: float32 [32, 256], P(('groups', 'dp')), parts along dimension 0
The draws below stay inside these ranges and needn't reach their ends.
There are 2 independent parts, one for each index of `groups`. The reference program is written for one: setup_inputs(seed, part) draws one part's arguments, and reference() takes and returns one part's arrays. A program takes and returns all parts, laid end to end along the dimension named above; an argument that names none is the same for every part. Nothing has to cross between parts.
All inputs are finite; a program needn't handle non-finite values.
Results may differ from the reference program's by a relative error of at most 0.0043.
Values may be sent and summed in bfloat16 or wider, within the bound.
A program may use at most 128 MiB of HBM per device.

```python
import jax
import jax.numpy as jnp
from jax import lax

D = 8192
R = 256
SEG_LEN = 256
DEPTHS = 8
SEGS = 16
TOKENS = 4096


def touch_ends(result, key, least, top_value):
    longest = result.shape.index(max(result.shape))
    spots = []
    for shift in (0, 1):
        where = [jax.random.randint(jax.random.fold_in(key, axis), (), 0, length) for axis, length in enumerate(result.shape)]
        where[longest] = (where[longest] + shift) % result.shape[longest]
        spots.append(tuple(where))
    return result.at[spots[0]].set(least).at[spots[1]].set(top_value)


def block_scale(stream_key, shape, cuts, least, largest):
    factor_of = 1.0
    for axis_at, shards_of in cuts:
        heights = jax.random.uniform(jax.random.fold_in(jax.random.fold_in(stream_key, 6), axis_at), (shards_of,), jnp.float32, least / len(cuts), largest / len(cuts))
        factor_of = factor_of * jnp.repeat(jnp.exp(heights), shape[axis_at] // shards_of).reshape((-1,) + (1,) * (len(shape) - 1 - axis_at))
    return factor_of


def bell_draw(own_key, extent, spread, bound, pieces=(), kind=jnp.bfloat16):
    level = block_scale(own_key, extent, pieces, -0.22, 0.18) if pieces else 1.0
    values = jax.random.normal(own_key, extent, jnp.float32) * spread * level
    return jnp.minimum(jnp.maximum(values, -bound), bound).astype(kind)


def setup_inputs(seed: int = 0, part: int = 0) -> dict:
    arg_keys = jax.random.split(jax.random.key(seed), 9)
    part_splits = jax.random.split(jax.random.fold_in(arg_keys[8], part), 9)
    return {
        "tokens": bell_draw(part_splits[0], (TOKENS, D), 1.0, 6.0, ((0, 16),)),
        "chosen_rows": bell_draw(part_splits[1], (TOKENS, D), D ** -0.5, 0.0625, ((0, 16),)),
        "adapter_down": bell_draw(arg_keys[2], (D, R), D ** -0.5, 0.0625, ((0, 16),)),
        "adapter_up": bell_draw(arg_keys[3], (R, D), R ** -0.5, 0.375, ((1, 16),)),
        "lengths": touch_ends(jax.random.randint(part_splits[4], (SEGS,), 1, SEG_LEN + 1), jax.random.fold_in(part_splits[4], 1), 1, SEG_LEN).astype(jnp.int32),
        "parent": touch_ends(jax.random.randint(part_splits[5], (SEGS,), 0, SEGS // 2), jax.random.fold_in(part_splits[5], 1), 0, (SEGS // 2) - 1).astype(jnp.int32),
        "depth": touch_ends(jax.random.randint(part_splits[6], (SEGS,), 0, DEPTHS), jax.random.fold_in(part_splits[6], 1), 0, DEPTHS - 1).astype(jnp.int32),
        "reward": bell_draw(part_splits[7], (SEGS,), 1.0, 6.0, ((0, 16),), jnp.float32),
    }


def reference(tokens, chosen_rows, adapter_down, adapter_up, lengths, parent, depth, reward):
    latent = jnp.dot(tokens, adapter_down, preferred_element_type=jnp.float32).astype(jnp.bfloat16)

    def seg_score(items):
        tok, chosen, lat = items
        mixed = tok.astype(jnp.float32) + jnp.dot(lat, adapter_up, preferred_element_type=jnp.float32)
        return lax.optimization_barrier(jnp.sum(mixed * chosen.astype(jnp.float32), axis=1))
    score = lax.map(seg_score, (tokens.reshape(SEGS, SEG_LEN, D), chosen_rows.reshape(SEGS, SEG_LEN, D), latent.reshape(SEGS, SEG_LEN, R)))
    position = lax.broadcasted_iota(jnp.int32, (SEGS, SEG_LEN), 1)
    valid = (position < lengths[:, None]).astype(jnp.float32)
    masked = score * valid
    parent_hot = (parent[None, :] == jnp.arange(SEGS, dtype=jnp.int32)[:, None]).astype(jnp.float32)
    depth_hot = (depth[None, :] == jnp.arange(DEPTHS, dtype=jnp.int32)[:, None]).astype(jnp.float32)
    high = lax.Precision.HIGHEST
    group_sum = jnp.dot(parent_hot, masked, precision=high)
    group_count = lax.optimization_barrier(jnp.sum(parent_hot, axis=1))
    sibling_mean = group_sum / jnp.maximum(group_count, 1.0)[:, None]
    depth_sum = jnp.dot(depth_hot, masked, precision=high)
    depth_count = lax.optimization_barrier(jnp.sum(depth_hot, axis=1))
    depth_mean = depth_sum / jnp.maximum(depth_count, 1.0)[:, None]
    own_sibling = jnp.dot(parent_hot.T, sibling_mean, precision=high)
    own_depth = jnp.dot(depth_hot.T, depth_mean, precision=high)
    advantage = (reward[:, None] + masked - own_sibling - 0.5 * own_depth) * valid
    weight = -advantage.reshape(-1)
    slope = (weight[:, None] * chosen_rows.astype(jnp.float32)).astype(jnp.bfloat16)
    latent_grad = lax.dot_general(slope, adapter_up, (((1,), (1,)), ((), ())), preferred_element_type=jnp.float32).astype(jnp.bfloat16)
    scale = 1.0 / jnp.sqrt(jnp.float32(TOKENS))
    grad_up = lax.dot_general(latent, slope, (((0,), (0,)), ((), ())), preferred_element_type=jnp.float32) * scale
    grad_down = lax.dot_general(tokens, latent_grad, (((0,), (0,)), ((), ())), preferred_element_type=jnp.float32) * scale
    return (grad_down, grad_up, advantage)
```

```python
import functools

import jax
import jax.numpy as jnp
from jax import lax
from jax.experimental import pallas as pl
from jax.experimental.pallas import tpu as pltpu
from jax.sharding import PartitionSpec as P

MESH = pl.DeviceIdType.MESH
F32 = jnp.float32
BF16 = jnp.bfloat16
NT = (((1,), (1,)), ((), ()))
HALVES = 2


def chip_of(pos, n):
    if n != 8:
        return pos
    side = pos // 4
    return 2 * (pos + side * (7 - 2 * pos)) + side


def pos_of(chip, n):
    if n != 8:
        return chip
    side, height = chip % 2, chip // 2
    return height + side * (7 - 2 * height)


def kernel(
    n,
    tok, cho, down, up, lengths, parent, depth, reward,
    o_down, o_up, o_adv,
    X, C, S, Wd, Wu, lat_a, lat_b, q_a, ts, lg_a, lg_b, lhs_u, lhs_d, wcol, msg,
    st_u, rc_u, st_d, rc_d,
    s_x, s_w, s_xs, s_xr, s_ags, s_agr, s_pair_s, s_pair_r, s_ms, s_mr, s_rs, s_rr,
):
    T, R, bw = tok.shape[0], down.shape[1], down.shape[0]
    ndp = 2 * n
    me = lax.axis_index("dp")
    core, p = me % 2, pos_of(me // 2, n)
    sib = me + 1 - 2 * core
    hb, hs = n // 2, n // 2 - 1

    def at(k):
        return (p + k + 2 * n) % n

    def dev(pos, c):
        return 2 * chip_of(pos, n) + c

    def cols(pos, c):
        return pl.ds(pl.multiple_of(dev(pos, c) * bw, bw), bw)

    right, left = dev(at(1), core), dev(at(-1), core)
    mine = pl.ds(pl.multiple_of(core * T, T), T)

    def remote(src, dst, ss, rs, target):
        return pltpu.make_async_remote_copy(
            src_ref=src, dst_ref=dst, send_sem=ss, recv_sem=rs,
            device_id={"dp": target}, device_id_type=MESH,
        )

    w_local = [
        pltpu.make_async_copy(down, Wd.at[p], s_w.at[0]),
        pltpu.make_async_copy(up, Wu.at[p], s_w.at[1]),
    ]
    for cp in w_local:
        cp.start()

    barrier = pltpu.get_barrier_semaphore()

    @pl.loop(1, ndp)
    def _(o):
        pl.semaphore_signal(
            barrier, inc=1, device_id={"dp": (me + o) % ndp}, device_id_type=MESH
        )

    def x_local(k):
        pos = at(k)
        return [
            pltpu.make_async_copy(tok.at[:, cols(pos, core)], X.at[pos, mine], s_x.at[0, pos]),
            pltpu.make_async_copy(cho.at[:, cols(pos, core)], C.at[pos, mine], s_x.at[1, pos]),
        ]

    def x_pair(k):
        pos = at(k)
        return [
            remote(tok.at[:, cols(pos, 1 - core)], X.at[pos, mine], s_xs.at[0, pos], s_xr.at[0, pos], sib),
            remote(cho.at[:, cols(pos, 1 - core)], C.at[pos, mine], s_xs.at[1, pos], s_xr.at[1, pos], sib),
        ]

    order = [0]
    for s in range(1, hb + 1):
        order += [-s] if s == hb else [-s, s]
    for k in order:
        for cp in x_local(k):
            cp.start()
    pl.semaphore_wait(barrier, ndp - 1)

    hops = {0: (hb, hs), 1: (hs, hb)}

    def gather(arr, way, s):
        ref, own = ((Wd, down), (Wu, up))[arr]
        pos = at(-s if way == 0 else s)
        src = own if s == 0 else ref.at[pos]
        return remote(
            src, ref.at[pos], s_ags.at[arr, way, s], s_agr.at[arr, way, s], (right, left)[way]
        )

    def arrived(arr, way, s):
        ref = (Wd, Wu)[arr]
        pos = at(-(s + 1) if way == 0 else s + 1)
        return remote(
            ref.at[pos], ref.at[pos], s_ags.at[arr, way, s], s_agr.at[arr, way, s], (right, left)[way]
        )

    for arr in (0, 1):
        for way in (0, 1):
            gather(arr, way, 0).start()
    for k in order:
        for cp in x_pair(k):
            cp.start()

    lanes = 128

    def take_down(k, first=False):
        pos = at(k)
        x = X[pos]
        d = jnp.dot(x, Wd[pos], preferred_element_type=F32)
        lat_a[...] = d if first else lat_a[...] + d

    def take_up(k, first=False):
        pos = at(k)
        d = lax.dot_general(C[pos], Wu[pos], NT, preferred_element_type=F32)
        q_a[...] = d if first else q_a[...] + d

    def take_x(k, first=False):
        pos = at(k)
        t = jnp.zeros((2 * T, lanes), F32) if first else ts[...]
        for j in range(0, bw, lanes):
            sl = slice(j, j + lanes)
            t = t + X[pos, :, sl].astype(F32) * C[pos, :, sl].astype(F32)
        ts[...] = t

    def ready(k):
        for cp in x_local(k):
            cp.wait()
        for cp in x_pair(k):
            cp.wait_recv()

    for cp in w_local:
        cp.wait()
    ready(0)
    take_x(0, True)
    take_down(0, True)
    take_up(0, True)

    def pass_on(arr, s):
        got = []
        for way in (0, 1):
            if s - 1 < hops[arr][way]:
                arrived(arr, way, s - 1).wait_recv()
                if s < hops[arr][way]:
                    gather(arr, way, s).start()
                got.append(-s if way == 0 else s)
        return got

    pair_lat = remote(lat_a, lat_b, s_pair_s.at[0], s_pair_r.at[0], sib)
    for s in range(1, hb + 1):
        xs = [-s] if s == hb else [-s, s]
        for k in xs:
            ready(k)
            take_x(k)
        got = pass_on(0, s)
        for k in got:
            take_down(k)
        if s == hb:
            pair_lat.start()
        got = pass_on(1, s)
        for k in got:
            take_up(k)
    pair_lat.wait()
    lat = (lat_a[...] + lat_b[...]).astype(BF16).astype(F32)
    lhs_u[...] = lat.T.astype(BF16)

    prod = lat * q_a[...]
    t = ts[...]
    for j in range(0, R, lanes):
        t = t + prod[:, j : j + lanes]
    row = jnp.sum(t.T, axis=0, keepdims=True)
    msg[me, 0:1, :] = row[:, :T]
    msg[me, 1:2, :] = row[:, T:]
    ones = jnp.ones((1, T), F32)
    msg[me, 2:3, :] = ones * lengths[0].astype(F32)
    msg[me, 3:4, :] = ones * parent[0].astype(F32)
    msg[me, 4:5, :] = ones * depth[0].astype(F32)
    msg[me, 5:6, :] = ones * reward[0]
    msg[me, 6:8, :] = jnp.zeros((2, T), F32)

    def tell(o):
        return remote(msg.at[me], msg.at[me], s_ms.at[o], s_mr.at[me], (me + o) % ndp)

    def told(o):
        d = (me + o) % ndp
        return remote(msg.at[d], msg.at[d], s_ms.at[o], s_mr.at[d], d)

    @pl.loop(1, ndp)
    def _(o):
        tell(o).start()

    @pl.loop(1, ndp)
    def _(o):
        told(o).wait_recv()

    position = lax.broadcasted_iota(jnp.int32, (1, T), 1).astype(F32)
    base = me - core
    own = [msg[base], msg[base + 1]]
    zero = jnp.zeros((1, T), F32)
    sums = [[zero] * 4, [zero] * 4]
    for q in range(n):
        pair = [msg[2 * q], msg[2 * q + 1]]
        for c in (0, 1):
            score = pair[0][c : c + 1] + pair[1][c : c + 1]
            seg = pair[c]
            masked = jnp.where(position < seg[2:3], score, 0.0)
            for k in (0, 1):
                same_p = seg[3:4] == own[k][3:4]
                same_d = seg[4:5] == own[k][4:5]
                a = sums[k]
                sums[k] = [
                    a[0] + jnp.where(same_p, masked, 0.0),
                    a[1] + jnp.where(same_p, 1.0, 0.0),
                    a[2] + jnp.where(same_d, masked, 0.0),
                    a[3] + jnp.where(same_d, 1.0, 0.0),
                ]
    adv = []
    for k in (0, 1):
        score = own[0][k : k + 1] + own[1][k : k + 1]
        valid = position < own[k][2:3]
        masked = jnp.where(valid, score, 0.0)
        a = sums[k]
        val = (
            own[k][5:6] + masked
            - a[0] / jnp.maximum(a[1], 1.0)
            - 0.5 * (a[2] / jnp.maximum(a[3], 1.0))
        )
        adv.append(jnp.where(valid, val, 0.0))
    o_adv[...] = jnp.where(core == 0, adv[0], adv[1])
    weight = -jnp.concatenate(adv, axis=1)
    wcol[...] = jnp.broadcast_to(weight, (lanes, 2 * T)).T

    def slope(k):
        pos = at(k)
        for j in range(0, bw, lanes):
            sl = slice(j, j + lanes)
            S[pos, :, sl] = (wcol[...] * C[pos, :, sl].astype(F32)).astype(BF16)

    rows = R // HALVES
    rs_hops = {0: (hb, hs), 1: (hs, hb)}
    stage, landed = (st_u, st_d), (rc_u, rc_d)
    lhs, rhs = (lhs_u, lhs_d), (S, X)

    def partial(arr, pos, h):
        return jnp.dot(
            lhs[arr][h * rows : (h + 1) * rows, :], rhs[arr][pos], preferred_element_type=F32
        )

    def rs_copy(arr, way, s, h):
        slot = s if way == 0 else rs_hops[arr][0] + s
        part = pl.ds(h * rows, rows)
        return remote(
            stage[arr].at[slot, part], landed[arr].at[slot, part],
            s_rs.at[arr, slot, h], s_rr.at[arr, slot, h], (right, left)[way],
        )

    def rs_step(arr, s):
        for h in range(HALVES):
            part = slice(h * rows, (h + 1) * rows)
            for way in (0, 1):
                count = rs_hops[arr][way]
                if s >= count:
                    continue
                off = rs_hops[arr][0]
                slot = s if way == 0 else off + s
                pos = at(count - s if way == 0 else s - count)
                val = partial(arr, pos, h)
                if s > 0:
                    rs_copy(arr, way, s - 1, h).wait_recv()
                    val = val + landed[arr][slot - 1, part, :].astype(F32)
                stage[arr][slot, part, :] = val.astype(stage[arr].dtype)
                rs_copy(arr, way, s, h).start()

    def rs_end(arr):
        off = rs_hops[arr][0]
        for h in range(HALVES):
            part = slice(h * rows, (h + 1) * rows)
            val = partial(arr, p, h)
            for way in (1, 0) if rs_hops[arr][1] < off else (0, 1):
                last = rs_hops[arr][way] - 1
                rs_copy(arr, way, last, h).wait_recv()
                val = val + landed[arr][last if way == 0 else off + last, part, :].astype(F32)
            if arr == 0:
                o_up[part, :] = val
            else:
                o_down[:, part] = val.T

    slope(hb)
    slope(-hs)
    rs_step(0, 0)
    for k in range(-hs + 1, hb):
        slope(k)
    for k in range(n):
        d = lax.dot_general(S[k], Wu[k], NT, preferred_element_type=F32)
        lg_a[...] = d if k == 0 else lg_a[...] + d
    pair_lg = remote(lg_a, lg_b, s_pair_s.at[1], s_pair_r.at[1], sib)
    pair_lg.start()
    rs_step(0, 1)
    pair_lg.wait()
    lhs_d[...] = (lg_a[...] + lg_b[...]).T.astype(BF16)
    rs_step(1, 0)
    for s in range(2, hb):
        rs_step(0, s)
        rs_step(1, s - 1)
    rs_end(0)
    rs_step(1, hb - 1)
    rs_end(1)

    for k in order:
        for cp in x_pair(k):
            cp.wait_send()
    for arr in (0, 1):
        for way in (0, 1):
            for s in range(hops[arr][way]):
                gather(arr, way, s).wait_send()
            for s in range(rs_hops[arr][way]):
                for h in range(HALVES):
                    rs_copy(arr, way, s, h).wait_send()

    @pl.loop(1, ndp)
    def _(o):
        tell(o).wait_send()


def solution(mesh):
    ndp = mesh.shape["dp"]
    n = ndp // 2
    wire = BF16 if n <= 8 else F32

    def body(tokens, chosen_rows, adapter_down, adapter_up, lengths, parent, depth, reward):
        T, D = tokens.shape
        bw, R = adapter_down.shape
        hb = n // 2
        dma, vm = pltpu.SemaphoreType.DMA, pltpu.VMEM
        hbm = pl.BlockSpec(memory_space=pltpu.HBM)
        smem = pl.BlockSpec(memory_space=pltpu.SMEM)
        vmem = pl.BlockSpec(memory_space=pltpu.VMEM)
        g_down, g_up, adv = pl.pallas_call(
            functools.partial(kernel, n),
            out_shape=(
                jax.ShapeDtypeStruct((bw, R), F32),
                jax.ShapeDtypeStruct((R, bw), F32),
                jax.ShapeDtypeStruct((1, T), F32),
            ),
            in_specs=[hbm] * 4 + [smem] * 4,
            out_specs=(vmem,) * 3,
            scratch_shapes=[
                vm((n, 2 * T, bw), BF16),
                vm((n, 2 * T, bw), BF16),
                vm((n, 2 * T, bw), BF16),
                vm((n, bw, R), BF16),
                vm((n, R, bw), BF16),
                vm((2 * T, R), F32),
                vm((2 * T, R), F32),
                vm((2 * T, R), F32),
                vm((2 * T, 128), F32),
                vm((2 * T, R), F32),
                vm((2 * T, R), F32),
                vm((R, 2 * T), BF16),
                vm((R, 2 * T), BF16),
                vm((2 * T, 128), F32),
                vm((ndp, 8, T), F32),
                vm((n - 1, R, bw), wire),
                vm((n - 1, R, bw), wire),
                vm((n - 1, R, bw), wire),
                vm((n - 1, R, bw), wire),
                dma((2, n)),
                dma((2,)),
                dma((2, n)),
                dma((2, n)),
                dma((2, 2, hb)),
                dma((2, 2, hb)),
                dma((2,)),
                dma((2,)),
                dma((ndp,)),
                dma((ndp,)),
                dma((2, n - 1, HALVES)),
                dma((2, n - 1, HALVES)),
            ],
            compiler_params=pltpu.CompilerParams(
                collective_id=0, has_side_effects=True, vmem_limit_bytes=56 * 1024 * 1024
            ),
            cost_estimate=pl.CostEstimate(
                flops=10 * T * D * R, bytes_accessed=4 * T * D, transcendentals=0
            ),
        )(tokens, chosen_rows, adapter_down, adapter_up, lengths, parent, depth, reward)
        scale = 1.0 / jnp.sqrt(jnp.float32(T * ndp))
        return g_down * scale, g_up * scale, adv

    in_specs = (
        P(("groups", "dp"), None),
        P(("groups", "dp"), None),
        P("dp", None),
        P(None, "dp"),
        P(("groups", "dp")),
        P(("groups", "dp")),
        P(("groups", "dp")),
        P(("groups", "dp")),
    )
    out_specs = (P(("groups", "dp"), None), P("groups", "dp"), P(("groups", "dp"), None))
    return jax.shard_map(body, mesh=mesh, in_specs=in_specs, out_specs=out_specs, check_vma=False)
```

```python
import functools
import math

import jax
import jax.numpy as jnp
from jax import lax
from jax.experimental import pallas as pl
from jax.experimental.pallas import tpu as pltpu
from jax.sharding import PartitionSpec as P

MESH = pl.DeviceIdType.MESH
F32 = jnp.float32
BF16 = jnp.bfloat16
NT = (((1,), (1,)), ((), ()))
HALVES = 2


def chip_of(pos, n):
    if n != 8:
        return pos
    side = pos // 4
    return 2 * (pos + side * (7 - 2 * pos)) + side


def pos_of(chip, n):
    if n != 8:
        return chip
    side, height = chip % 2, chip // 2
    return height + side * (7 - 2 * height)


def kernel(
    n, scale,
    tok, cho, down, up, lengths, parent, depth, reward,
    o_down, o_up, o_adv,
    X, C, S, Wd, Wu, lat_a, lat_b, q_a, ts, lg_a, lg_b, lhs_u, lhs_d, wcol, msg,
    st_u, rc_u, st_d, rc_d,
    s_x, s_w, s_xs, s_xr, s_ags, s_agr, s_gs, s_gr, s_pair_s, s_pair_r, s_ms, s_mr, s_rs, s_rr,
):
    T, R, bw = tok.shape[0], down.shape[1], down.shape[0]
    ndp = 2 * n
    me = lax.axis_index("dp")
    core, p = me % 2, pos_of(me // 2, n)
    sib = me + 1 - 2 * core
    hb, hs = n // 2, n // 2 - 1
    group = lax.axis_index("groups")
    odd = group % 2
    other = group + 1 - 2 * odd

    def at(k):
        return (p + k + 2 * n) % n

    def dev(pos, c):
        return 2 * chip_of(pos, n) + c

    def cols(pos, c):
        return pl.ds(pl.multiple_of(dev(pos, c) * bw, bw), bw)

    right, left = dev(at(1), core), dev(at(-1), core)
    mine = pl.ds(pl.multiple_of(core * T, T), T)

    def remote(src, dst, ss, rs, target):
        return pltpu.make_async_remote_copy(
            src_ref=src, dst_ref=dst, send_sem=ss, recv_sem=rs,
            device_id={"dp": target}, device_id_type=MESH,
        )

    w_local = [
        pltpu.make_async_copy(down, Wd.at[p], s_w.at[0]),
        pltpu.make_async_copy(up, Wu.at[p], s_w.at[1]),
    ]
    for cp in w_local:
        cp.start()

    barrier = pltpu.get_barrier_semaphore()

    @pl.loop(1, ndp)
    def _(o):
        pl.semaphore_signal(
            barrier, inc=1, device_id={"dp": (me + o) % ndp}, device_id_type=MESH
        )

    pl.semaphore_signal(
        barrier, inc=1, device_id={"groups": other}, device_id_type=MESH
    )

    def x_local(k):
        pos = at(k)
        return [
            pltpu.make_async_copy(tok.at[:, cols(pos, core)], X.at[pos, mine], s_x.at[0, pos]),
            pltpu.make_async_copy(cho.at[:, cols(pos, core)], C.at[pos, mine], s_x.at[1, pos]),
        ]

    def x_pair(k):
        pos = at(k)
        return [
            remote(tok.at[:, cols(pos, 1 - core)], X.at[pos, mine], s_xs.at[0, pos], s_xr.at[0, pos], sib),
            remote(cho.at[:, cols(pos, 1 - core)], C.at[pos, mine], s_xs.at[1, pos], s_xr.at[1, pos], sib),
        ]

    order = [0]
    for s in range(1, hb + 1):
        order += [-s] if s == hb else [-s, s]
    for k in order:
        for cp in x_local(k):
            cp.start()
    pl.semaphore_wait(barrier, ndp)

    hops = {0: (hb, hs), 1: (hs, hb)}

    quarter = (bw // 4, R // 4)

    def ringed(arr):
        m = quarter[arr]
        return pl.ds(pl.multiple_of(odd * m, m), 3 * m)

    def across(arr, way, s, side):
        ref, m = (Wd, Wu)[arr], quarter[arr]
        pos = at(-(s + 1) if way == 0 else s + 1)
        part = pl.ds(pl.multiple_of(side * 3 * m, m), m)
        return pltpu.make_async_remote_copy(
            src_ref=ref.at[pos, part], dst_ref=ref.at[pos, part],
            send_sem=s_gs.at[arr, way, s], recv_sem=s_gr.at[arr, way, s],
            device_id={"groups": other}, device_id_type=MESH,
        )

    def gather(arr, way, s):
        ref, own = ((Wd, down), (Wu, up))[arr]
        pos = at(-s if way == 0 else s)
        part = ringed(arr)
        src = own.at[part] if s == 0 else ref.at[pos, part]
        return remote(
            src, ref.at[pos, part], s_ags.at[arr, way, s], s_agr.at[arr, way, s], (right, left)[way]
        )

    def arrived(arr, way, s):
        ref = (Wd, Wu)[arr]
        pos = at(-(s + 1) if way == 0 else s + 1)
        part = ringed(arr)
        return remote(
            ref.at[pos, part], ref.at[pos, part], s_ags.at[arr, way, s], s_agr.at[arr, way, s], (right, left)[way]
        )

    for arr in (0, 1):
        for way in (0, 1):
            gather(arr, way, 0).start()
    for k in order:
        for cp in x_pair(k):
            cp.start()

    lanes = 128

    def take_down(k, first=False):
        pos = at(k)
        x = X[pos]
        d = jnp.dot(x, Wd[pos], preferred_element_type=F32)
        lat_a[...] = d if first else lat_a[...] + d

    def take_up(k, first=False):
        pos = at(k)
        d = lax.dot_general(C[pos], Wu[pos], NT, preferred_element_type=F32)
        q_a[...] = d if first else q_a[...] + d

    def take_x(k, first=False):
        pos = at(k)
        t = jnp.zeros((2 * T, lanes), F32) if first else ts[...]
        for j in range(0, bw, lanes):
            sl = slice(j, j + lanes)
            t = t + X[pos, :, sl].astype(F32) * C[pos, :, sl].astype(F32)
        ts[...] = t

    def ready(k):
        for cp in x_local(k):
            cp.wait()
        for cp in x_pair(k):
            cp.wait_recv()

    for cp in w_local:
        cp.wait()
    ready(0)
    take_x(0, True)
    take_down(0, True)
    take_up(0, True)

    def pass_on(arr, s):
        for way in (0, 1):
            if s - 1 < hops[arr][way]:
                arrived(arr, way, s - 1).wait_recv()
                if s < hops[arr][way]:
                    gather(arr, way, s).start()
                across(arr, way, s - 1, odd).start()

    def take(arr, s):
        for way in (0, 1):
            if s - 1 < hops[arr][way]:
                across(arr, way, s - 1, 1 - odd).wait_recv()
                (take_down, take_up)[arr](-s if way == 0 else s)

    pair_lat = remote(lat_a, lat_b, s_pair_s.at[0], s_pair_r.at[0], sib)
    for s in range(1, hb + 1):
        xs = [-s] if s == hb else [-s, s]
        for k in xs:
            ready(k)
            take_x(k)
        pass_on(0, s)
        if s > 1:
            take(0, s - 1)
        if s == hb:
            take(0, s)
            pair_lat.start()
        pass_on(1, s)
        if s > 1:
            take(1, s - 1)
    take(1, hb)
    pair_lat.wait()
    lat = (lat_a[...] + lat_b[...]).astype(BF16).astype(F32)
    lhs_u[...] = lat.T.astype(BF16)

    prod = lat * q_a[...]
    t = ts[...]
    for j in range(0, R, lanes):
        t = t + prod[:, j : j + lanes]
    row = jnp.sum(t.T, axis=0, keepdims=True)
    msg[me, 0:1, :] = row[:, :T]
    msg[me, 1:2, :] = row[:, T:]
    ones = jnp.ones((1, T), F32)
    msg[me, 2:3, :] = ones * lengths[0].astype(F32)
    msg[me, 3:4, :] = ones * parent[0].astype(F32)
    msg[me, 4:5, :] = ones * depth[0].astype(F32)
    msg[me, 5:6, :] = ones * reward[0]
    msg[me, 6:8, :] = jnp.zeros((2, T), F32)

    def tell(o):
        return remote(msg.at[me], msg.at[me], s_ms.at[o], s_mr.at[me], (me + o) % ndp)

    def told(o):
        d = (me + o) % ndp
        return remote(msg.at[d], msg.at[d], s_ms.at[o], s_mr.at[d], d)

    @pl.loop(1, ndp)
    def _(o):
        tell(o).start()

    @pl.loop(1, ndp)
    def _(o):
        told(o).wait_recv()

    position = lax.broadcasted_iota(jnp.int32, (1, T), 1).astype(F32)
    base = me - core
    own = [msg[base], msg[base + 1]]
    zero = jnp.zeros((1, T), F32)
    sums = [[zero] * 4, [zero] * 4]
    for q in range(n):
        pair = [msg[2 * q], msg[2 * q + 1]]
        for c in (0, 1):
            score = pair[0][c : c + 1] + pair[1][c : c + 1]
            seg = pair[c]
            masked = jnp.where(position < seg[2:3], score, 0.0)
            for k in (0, 1):
                same_p = seg[3:4] == own[k][3:4]
                same_d = seg[4:5] == own[k][4:5]
                a = sums[k]
                sums[k] = [
                    a[0] + jnp.where(same_p, masked, 0.0),
                    a[1] + jnp.where(same_p, 1.0, 0.0),
                    a[2] + jnp.where(same_d, masked, 0.0),
                    a[3] + jnp.where(same_d, 1.0, 0.0),
                ]
    adv = []
    for k in (0, 1):
        score = own[0][k : k + 1] + own[1][k : k + 1]
        valid = position < own[k][2:3]
        masked = jnp.where(valid, score, 0.0)
        a = sums[k]
        val = (
            own[k][5:6] + masked
            - a[0] / jnp.maximum(a[1], 1.0)
            - 0.5 * (a[2] / jnp.maximum(a[3], 1.0))
        )
        adv.append(jnp.where(valid, val, 0.0))
    o_adv[...] = jnp.where(core == 0, adv[0], adv[1])
    weight = -jnp.concatenate(adv, axis=1)
    wcol[...] = jnp.broadcast_to(weight, (lanes, 2 * T)).T

    def slope(k):
        pos = at(k)
        for j in range(0, bw, lanes):
            sl = slice(j, j + lanes)
            S[pos, :, sl] = (wcol[...] * C[pos, :, sl].astype(F32)).astype(BF16)

    rows = R // HALVES
    rs_hops = {0: (hb, hs), 1: (hs, hb)}
    stage, landed = (st_u, st_d), (rc_u, rc_d)
    lhs, rhs = (lhs_u, lhs_d), (S, X)

    def partial(arr, pos, h):
        return jnp.dot(
            lhs[arr][h * rows : (h + 1) * rows, :], rhs[arr][pos], preferred_element_type=F32
        )

    def rs_copy(arr, way, s, h):
        slot = s if way == 0 else rs_hops[arr][0] + s
        part = pl.ds(h * rows, rows)
        return remote(
            stage[arr].at[slot, part], landed[arr].at[slot, part],
            s_rs.at[arr, slot, h], s_rr.at[arr, slot, h], (right, left)[way],
        )

    def rs_step(arr, s):
        for h in range(HALVES):
            part = slice(h * rows, (h + 1) * rows)
            for way in (0, 1):
                count = rs_hops[arr][way]
                if s >= count:
                    continue
                off = rs_hops[arr][0]
                slot = s if way == 0 else off + s
                pos = at(count - s if way == 0 else s - count)
                val = partial(arr, pos, h)
                if s > 0:
                    rs_copy(arr, way, s - 1, h).wait_recv()
                    val = val + landed[arr][slot - 1, part, :].astype(F32)
                stage[arr][slot, part, :] = val.astype(stage[arr].dtype)
                rs_copy(arr, way, s, h).start()

    def rs_end(arr):
        off = rs_hops[arr][0]
        for h in range(HALVES):
            part = slice(h * rows, (h + 1) * rows)
            val = partial(arr, p, h)
            for way in (1, 0) if rs_hops[arr][1] < off else (0, 1):
                last = rs_hops[arr][way] - 1
                rs_copy(arr, way, last, h).wait_recv()
                val = val + landed[arr][last if way == 0 else off + last, part, :].astype(F32)
            if arr == 0:
                o_up[part, :] = val * scale
            else:
                o_down[:, part] = (val * scale).T

    slope(hb)
    slope(-hs)
    rs_step(0, 0)
    for k in range(-hs + 1, hb):
        slope(k)
    for k in range(n):
        d = lax.dot_general(S[k], Wu[k], NT, preferred_element_type=F32)
        lg_a[...] = d if k == 0 else lg_a[...] + d
    pair_lg = remote(lg_a, lg_b, s_pair_s.at[1], s_pair_r.at[1], sib)
    pair_lg.start()
    rs_step(0, 1)
    pair_lg.wait()
    lhs_d[...] = (lg_a[...] + lg_b[...]).T.astype(BF16)
    rs_step(1, 0)
    for s in range(2, hb):
        rs_step(0, s)
        rs_step(1, s - 1)
    rs_end(0)
    rs_step(1, hb - 1)
    rs_end(1)

    for k in order:
        for cp in x_pair(k):
            cp.wait_send()
    for arr in (0, 1):
        for way in (0, 1):
            for s in range(hops[arr][way]):
                gather(arr, way, s).wait_send()
                across(arr, way, s, odd).wait_send()
            for s in range(rs_hops[arr][way]):
                for h in range(HALVES):
                    rs_copy(arr, way, s, h).wait_send()

    @pl.loop(1, ndp)
    def _(o):
        tell(o).wait_send()


def solution(mesh):
    ndp = mesh.shape["dp"]
    n = ndp // 2
    wire = BF16 if n <= 8 else F32

    def body(tokens, chosen_rows, adapter_down, adapter_up, lengths, parent, depth, reward):
        T, D = tokens.shape
        bw, R = adapter_down.shape
        hb = n // 2
        dma, vm = pltpu.SemaphoreType.DMA, pltpu.VMEM
        hbm = pl.BlockSpec(memory_space=pltpu.HBM)
        smem = pl.BlockSpec(memory_space=pltpu.SMEM)
        vmem = pl.BlockSpec(memory_space=pltpu.VMEM)
        scale = 1.0 / math.sqrt(T * ndp)
        return pl.pallas_call(
            functools.partial(kernel, n, scale),
            out_shape=(
                jax.ShapeDtypeStruct((bw, R), F32),
                jax.ShapeDtypeStruct((R, bw), F32),
                jax.ShapeDtypeStruct((1, T), F32),
            ),
            in_specs=[hbm] * 4 + [smem] * 4,
            out_specs=(vmem,) * 3,
            scratch_shapes=[
                vm((n, 2 * T, bw), BF16),
                vm((n, 2 * T, bw), BF16),
                vm((n, 2 * T, bw), BF16),
                vm((n, bw, R), BF16),
                vm((n, R, bw), BF16),
                vm((2 * T, R), F32),
                vm((2 * T, R), F32),
                vm((2 * T, R), F32),
                vm((2 * T, 128), F32),
                vm((2 * T, R), F32),
                vm((2 * T, R), F32),
                vm((R, 2 * T), BF16),
                vm((R, 2 * T), BF16),
                vm((2 * T, 128), F32),
                vm((ndp, 8, T), F32),
                vm((n - 1, R, bw), wire),
                vm((n - 1, R, bw), wire),
                vm((n - 1, R, bw), wire),
                vm((n - 1, R, bw), wire),
                dma((2, n)),
                dma((2,)),
                dma((2, n)),
                dma((2, n)),
                dma((2, 2, hb)),
                dma((2, 2, hb)),
                dma((2, 2, hb)),
                dma((2, 2, hb)),
                dma((2,)),
                dma((2,)),
                dma((ndp,)),
                dma((ndp,)),
                dma((2, n - 1, HALVES)),
                dma((2, n - 1, HALVES)),
            ],
            compiler_params=pltpu.CompilerParams(
                collective_id=0, has_side_effects=True, vmem_limit_bytes=56 * 1024 * 1024
            ),
            cost_estimate=pl.CostEstimate(
                flops=10 * T * D * R, bytes_accessed=4 * T * D, transcendentals=0
            ),
        )(tokens, chosen_rows, adapter_down, adapter_up, lengths, parent, depth, reward)

    in_specs = (
        P(("groups", "dp"), None),
        P(("groups", "dp"), None),
        P("dp", None),
        P(None, "dp"),
        P(("groups", "dp")),
        P(("groups", "dp")),
        P(("groups", "dp")),
        P(("groups", "dp")),
    )
    out_specs = (P(("groups", "dp"), None), P("groups", "dp"), P(("groups", "dp"), None))
    return jax.shard_map(body, mesh=mesh, in_specs=in_specs, out_specs=out_specs, check_vma=False)
```

```python
import functools
import math

import jax
import jax.numpy as jnp
from jax import lax
from jax.experimental import pallas as pl
from jax.experimental.pallas import tpu as pltpu
from jax.sharding import PartitionSpec as P

MESH = pl.DeviceIdType.MESH
F32 = jnp.float32
BF16 = jnp.bfloat16
NT = (((1,), (1,)), ((), ()))
HALVES = 2


def chip_of(pos, n):
    if n != 8:
        return pos
    side = pos // 4
    return 2 * (pos + side * (7 - 2 * pos)) + side


def pos_of(chip, n):
    if n != 8:
        return chip
    side, height = chip % 2, chip // 2
    return height + side * (7 - 2 * height)


def kernel(
    n, scale,
    tok, cho, down, up, lengths, parent, depth, reward,
    o_down, o_up, o_adv,
    X, C, S, Wd, Wu, lat_a, lat_b, q_a, ts, lg_a, lg_b, lhs_u, lhs_d, wcol, msg,
    st_u, rc_u, st_d, rc_d,
    s_x, s_w, s_xs, s_xr, s_ags, s_agr, s_gs, s_gr, s_pair_s, s_pair_r, s_ms, s_mr, s_rs, s_rr,
):
    T, R, bw = tok.shape[0], down.shape[1], down.shape[0]
    ndp = 2 * n
    me = lax.axis_index("dp")
    core, p = me % 2, pos_of(me // 2, n)
    sib = me + 1 - 2 * core
    hb, hs = n // 2, n // 2 - 1
    group = lax.axis_index("groups")
    odd = group % 2
    other = group + 1 - 2 * odd

    def at(k):
        return (p + k + 2 * n) % n

    def dev(pos, c):
        return 2 * chip_of(pos, n) + c

    def cols(pos, c):
        return pl.ds(pl.multiple_of(dev(pos, c) * bw, bw), bw)

    right, left = dev(at(1), core), dev(at(-1), core)
    mine = pl.ds(pl.multiple_of(core * T, T), T)

    def remote(src, dst, ss, rs, target):
        return pltpu.make_async_remote_copy(
            src_ref=src, dst_ref=dst, send_sem=ss, recv_sem=rs,
            device_id={"dp": target}, device_id_type=MESH,
        )

    w_local = [
        pltpu.make_async_copy(down, Wd.at[p], s_w.at[0]),
        pltpu.make_async_copy(up, Wu.at[p], s_w.at[1]),
    ]
    for cp in w_local:
        cp.start()

    barrier = pltpu.get_barrier_semaphore()

    @pl.loop(1, ndp)
    def _(o):
        pl.semaphore_signal(
            barrier, inc=1, device_id={"dp": (me + o) % ndp}, device_id_type=MESH
        )

    pl.semaphore_signal(
        barrier, inc=1, device_id={"groups": other}, device_id_type=MESH
    )

    def x_local(k):
        pos = at(k)
        return [
            pltpu.make_async_copy(tok.at[:, cols(pos, core)], X.at[pos, mine], s_x.at[0, pos]),
            pltpu.make_async_copy(cho.at[:, cols(pos, core)], C.at[pos, mine], s_x.at[1, pos]),
        ]

    def x_pair(k):
        pos = at(k)
        return [
            remote(tok.at[:, cols(pos, 1 - core)], X.at[pos, mine], s_xs.at[0, pos], s_xr.at[0, pos], sib),
            remote(cho.at[:, cols(pos, 1 - core)], C.at[pos, mine], s_xs.at[1, pos], s_xr.at[1, pos], sib),
        ]

    order = [0]
    for s in range(1, hb + 1):
        order += [-s] if s == hb else [-s, s]
    for k in order:
        for cp in x_local(k):
            cp.start()
    pl.semaphore_wait(barrier, ndp)

    hops = {0: (hb, hs), 1: (hs, hb)}

    quarter = (bw // 4, R // 4)

    def ringed(arr):
        m = quarter[arr]
        return pl.ds(pl.multiple_of(odd * m, m), 3 * m)

    def across(arr, way, s, side):
        ref, m = (Wd, Wu)[arr], quarter[arr]
        pos = at(-(s + 1) if way == 0 else s + 1)
        part = pl.ds(pl.multiple_of(side * 3 * m, m), m)
        return pltpu.make_async_remote_copy(
            src_ref=ref.at[pos, part], dst_ref=ref.at[pos, part],
            send_sem=s_gs.at[arr, way, s], recv_sem=s_gr.at[arr, way, s],
            device_id={"groups": other}, device_id_type=MESH,
        )

    def gather(arr, way, s):
        ref, own = ((Wd, down), (Wu, up))[arr]
        pos = at(-s if way == 0 else s)
        part = ringed(arr)
        src = own.at[part] if s == 0 else ref.at[pos, part]
        return remote(
            src, ref.at[pos, part], s_ags.at[arr, way, s], s_agr.at[arr, way, s], (right, left)[way]
        )

    def arrived(arr, way, s):
        ref = (Wd, Wu)[arr]
        pos = at(-(s + 1) if way == 0 else s + 1)
        part = ringed(arr)
        return remote(
            ref.at[pos, part], ref.at[pos, part], s_ags.at[arr, way, s], s_agr.at[arr, way, s], (right, left)[way]
        )

    for arr in (0, 1):
        for way in (0, 1):
            gather(arr, way, 0).start()
    for k in order:
        for cp in x_pair(k):
            cp.start()

    lanes = 128

    def take_down(k, first=False):
        pos = at(k)
        x = X[pos]
        d = jnp.dot(x, Wd[pos], preferred_element_type=F32)
        lat_a[...] = d if first else lat_a[...] + d

    def take_up(k, first=False):
        pos = at(k)
        d = lax.dot_general(C[pos], Wu[pos], NT, preferred_element_type=F32)
        q_a[...] = d if first else q_a[...] + d

    def take_x(k, first=False):
        pos = at(k)
        t = jnp.zeros((2 * T, lanes), F32) if first else ts[...]
        for j in range(0, bw, lanes):
            sl = slice(j, j + lanes)
            t = t + X[pos, :, sl].astype(F32) * C[pos, :, sl].astype(F32)
        ts[...] = t

    def ready(k):
        for cp in x_local(k):
            cp.wait()
        for cp in x_pair(k):
            cp.wait_recv()

    for cp in w_local:
        cp.wait()
    ready(0)
    take_x(0, True)
    take_down(0, True)
    take_up(0, True)

    def pass_on(arr, s):
        for way in (0, 1):
            if s - 1 < hops[arr][way]:
                arrived(arr, way, s - 1).wait_recv()
                if s < hops[arr][way]:
                    gather(arr, way, s).start()
                across(arr, way, s - 1, odd).start()

    def take(arr, s):
        for way in (0, 1):
            if s - 1 < hops[arr][way]:
                across(arr, way, s - 1, 1 - odd).wait_recv()
                (take_down, take_up)[arr](-s if way == 0 else s)

    pair_lat = remote(lat_a, lat_b, s_pair_s.at[0], s_pair_r.at[0], sib)
    for s in range(1, hb + 1):
        xs = [-s] if s == hb else [-s, s]
        for k in xs:
            ready(k)
            take_x(k)
        pass_on(0, s)
        if s > 1:
            take(0, s - 1)
        if s == hb:
            take(0, s)
            pair_lat.start()
        pass_on(1, s)
        if s > 1:
            take(1, s - 1)
    take(1, hb)
    pair_lat.wait()
    lat = (lat_a[...] + lat_b[...]).astype(BF16).astype(F32)
    lhs_u[...] = lat.T.astype(BF16)

    prod = lat * q_a[...]
    t = ts[...]
    for j in range(0, R, lanes):
        t = t + prod[:, j : j + lanes]
    row = jnp.sum(t.T, axis=0, keepdims=True)
    msg[me, 0:1, :] = row[:, :T]
    msg[me, 1:2, :] = row[:, T:]
    ones = jnp.ones((1, T), F32)
    msg[me, 2:3, :] = ones * lengths[0].astype(F32)
    msg[me, 3:4, :] = ones * parent[0].astype(F32)
    msg[me, 4:5, :] = ones * depth[0].astype(F32)
    msg[me, 5:6, :] = ones * reward[0]
    msg[me, 6:8, :] = jnp.zeros((2, T), F32)

    def tell(o):
        return remote(msg.at[me], msg.at[me], s_ms.at[o], s_mr.at[me], (me + o) % ndp)

    def told(o):
        d = (me + o) % ndp
        return remote(msg.at[d], msg.at[d], s_ms.at[o], s_mr.at[d], d)

    @pl.loop(1, ndp)
    def _(o):
        tell(o).start()

    @pl.loop(1, ndp)
    def _(o):
        told(o).wait_recv()

    position = lax.broadcasted_iota(jnp.int32, (1, T), 1).astype(F32)
    base = me - core
    own = [msg[base], msg[base + 1]]
    zero = jnp.zeros((1, T), F32)
    sums = [[zero] * 4, [zero] * 4]
    for q in range(n):
        pair = [msg[2 * q], msg[2 * q + 1]]
        for c in (0, 1):
            score = pair[0][c : c + 1] + pair[1][c : c + 1]
            seg = pair[c]
            masked = jnp.where(position < seg[2:3], score, 0.0)
            for k in (0, 1):
                same_p = seg[3:4] == own[k][3:4]
                same_d = seg[4:5] == own[k][4:5]
                a = sums[k]
                sums[k] = [
                    a[0] + jnp.where(same_p, masked, 0.0),
                    a[1] + jnp.where(same_p, 1.0, 0.0),
                    a[2] + jnp.where(same_d, masked, 0.0),
                    a[3] + jnp.where(same_d, 1.0, 0.0),
                ]
    adv = []
    for k in (0, 1):
        score = own[0][k : k + 1] + own[1][k : k + 1]
        valid = position < own[k][2:3]
        masked = jnp.where(valid, score, 0.0)
        a = sums[k]
        val = (
            own[k][5:6] + masked
            - a[0] / jnp.maximum(a[1], 1.0)
            - 0.5 * (a[2] / jnp.maximum(a[3], 1.0))
        )
        adv.append(jnp.where(valid, val, 0.0))
    o_adv[...] = jnp.where(core == 0, adv[0], adv[1])
    weight = -jnp.concatenate(adv, axis=1)
    wcol[...] = jnp.broadcast_to(weight, (lanes, 2 * T)).T

    def slope(k):
        pos = at(k)
        for j in range(0, bw, lanes):
            sl = slice(j, j + lanes)
            S[pos, :, sl] = (wcol[...] * C[pos, :, sl].astype(F32)).astype(BF16)

    rows = R // HALVES
    rs_hops = {0: (hb, hs), 1: (hs, hb)}
    stage, landed = (st_u, st_d), (rc_u, rc_d)
    lhs, rhs = (lhs_u, lhs_d), (S, X)

    def partial(arr, pos, h):
        return jnp.dot(
            lhs[arr][h * rows : (h + 1) * rows, :], rhs[arr][pos], preferred_element_type=F32
        )

    def rs_copy(arr, way, s, h):
        slot = s if way == 0 else rs_hops[arr][0] + s
        part = pl.ds(h * rows, rows)
        return remote(
            stage[arr].at[slot, part], landed[arr].at[slot, part],
            s_rs.at[arr, slot, h], s_rr.at[arr, slot, h], (right, left)[way],
        )

    def rs_step(arr, s):
        for h in range(HALVES):
            part = slice(h * rows, (h + 1) * rows)
            for way in (0, 1):
                count = rs_hops[arr][way]
                if s >= count:
                    continue
                off = rs_hops[arr][0]
                slot = s if way == 0 else off + s
                pos = at(count - s if way == 0 else s - count)
                val = partial(arr, pos, h)
                if s > 0:
                    rs_copy(arr, way, s - 1, h).wait_recv()
                    val = val + landed[arr][slot - 1, part, :].astype(F32)
                stage[arr][slot, part, :] = val.astype(stage[arr].dtype)
                rs_copy(arr, way, s, h).start()

    def rs_end(arr):
        off = rs_hops[arr][0]
        for h in range(HALVES):
            part = slice(h * rows, (h + 1) * rows)
            val = partial(arr, p, h)
            for way in (1, 0) if rs_hops[arr][1] < off else (0, 1):
                last = rs_hops[arr][way] - 1
                rs_copy(arr, way, last, h).wait_recv()
                val = val + landed[arr][last if way == 0 else off + last, part, :].astype(F32)
            if arr == 0:
                o_up[part, :] = val * scale
            else:
                o_down[:, part] = (val * scale).T

    slope(hb)
    slope(-hs)
    rs_step(0, 0)
    for k in range(-hs + 1, hb):
        slope(k)
    for k in range(n):
        d = lax.dot_general(S[k], Wu[k], NT, preferred_element_type=F32)
        lg_a[...] = d if k == 0 else lg_a[...] + d
    pair_lg = remote(lg_a, lg_b, s_pair_s.at[1], s_pair_r.at[1], sib)
    pair_lg.start()
    rs_step(0, 1)
    pair_lg.wait()
    lhs_d[...] = (lg_a[...] + lg_b[...]).T.astype(BF16)
    rs_step(1, 0)
    for s in range(2, hb):
        rs_step(0, s)
        rs_step(1, s - 1)
    rs_end(0)
    rs_step(1, hb - 1)
    rs_end(1)

    for k in order:
        for cp in x_pair(k):
            cp.wait_send()
    for arr in (0, 1):
        for way in (0, 1):
            for s in range(hops[arr][way]):
                gather(arr, way, s).wait_send()
                across(arr, way, s, odd).wait_send()
            for s in range(rs_hops[arr][way]):
                for h in range(HALVES):
                    rs_copy(arr, way, s, h).wait_send()

    @pl.loop(1, ndp)
    def _(o):
        tell(o).wait_send()


def solution(mesh):
    ndp = mesh.shape["dp"]
    n = ndp // 2
    wire = BF16 if n <= 8 else F32

    def body(tokens, chosen_rows, adapter_down, adapter_up, lengths, parent, depth, reward):
        T, D = tokens.shape
        bw, R = adapter_down.shape
        hb = n // 2
        dma, vm = pltpu.SemaphoreType.DMA, pltpu.VMEM
        hbm = pl.BlockSpec(memory_space=pltpu.HBM)
        smem = pl.BlockSpec(memory_space=pltpu.SMEM)
        vmem = pl.BlockSpec(memory_space=pltpu.VMEM)
        scale = 1.0 / math.sqrt(T * ndp)
        return pl.pallas_call(
            functools.partial(kernel, n, scale),
            out_shape=(
                jax.ShapeDtypeStruct((bw, R), F32),
                jax.ShapeDtypeStruct((R, bw), F32),
                jax.ShapeDtypeStruct((1, T), F32),
            ),
            in_specs=[hbm] * 4 + [smem] * 4,
            out_specs=(vmem,) * 3,
            scratch_shapes=[
                vm((n, 2 * T, bw), BF16),
                vm((n, 2 * T, bw), BF16),
                vm((n, 2 * T, bw), BF16),
                vm((n, bw, R), BF16),
                vm((n, R, bw), BF16),
                vm((2 * T, R), F32),
                vm((2 * T, R), F32),
                vm((2 * T, R), F32),
                vm((2 * T, 128), F32),
                vm((2 * T, R), F32),
                vm((2 * T, R), F32),
                vm((R, 2 * T), BF16),
                vm((R, 2 * T), BF16),
                vm((2 * T, 128), F32),
                vm((ndp, 8, T), F32),
                vm((n - 1, R, bw), wire),
                vm((n - 1, R, bw), wire),
                vm((n - 1, R, bw), wire),
                vm((n - 1, R, bw), wire),
                dma((2, n)),
                dma((2,)),
                dma((2, n)),
                dma((2, n)),
                dma((2, 2, hb)),
                dma((2, 2, hb)),
                dma((2, 2, hb)),
                dma((2, 2, hb)),
                dma((2,)),
                dma((2,)),
                dma((ndp,)),
                dma((ndp,)),
                dma((2, n - 1, HALVES)),
                dma((2, n - 1, HALVES)),
            ],
            compiler_params=pltpu.CompilerParams(
                collective_id=0, has_side_effects=True, vmem_limit_bytes=44 * 1024 * 1024
            ),
            cost_estimate=pl.CostEstimate(
                flops=10 * T * D * R, bytes_accessed=4 * T * D, transcendentals=0
            ),
        )(tokens, chosen_rows, adapter_down, adapter_up, lengths, parent, depth, reward)

    in_specs = (
        P(("groups", "dp"), None),
        P(("groups", "dp"), None),
        P("dp", None),
        P(None, "dp"),
        P(("groups", "dp")),
        P(("groups", "dp")),
        P(("groups", "dp")),
        P(("groups", "dp")),
    )
    out_specs = (P(("groups", "dp"), None), P("groups", "dp"), P(("groups", "dp"), None))
    return jax.shard_map(body, mesh=mesh, in_specs=in_specs, out_specs=out_specs, check_vma=False)
```
